128 devices in a mesh: atm: 16 (over z, y), ocn: 8 (over x, core).
Axes of the slice: x: 4, y: 4, z: 4, core: 2. Of those that a mesh axis runs over, the one named last changes fastest.
Arguments:
- atm_fields: bfloat16 [16384, 24, 128], P(('atm', 'ocn')), may hold values from -6 to 6
- fwd_blocks: bfloat16 [24576, 128, 128], P(('atm', 'ocn')), may hold values from -0.21875 to 0.21875
- fwd_src_tile: int32 [24576], P(('atm', 'ocn')), may hold values from 0 to 127
- fwd_dst_dev: int32 [24576, 1], P(('atm', 'ocn')), may hold values from 0 to 127, as said below
- fwd_dst_tile: int32 [24576], P(('atm', 'ocn')), may hold values from 0 to 7
- ocean_state: float32 [1024, 24, 128], P(('atm', 'ocn')), may hold values from -6 to 6
- wet_mask: int32 [1024, 128], P(('atm', 'ocn')), may hold values 0 or 1
- back_blocks: bfloat16 [24576, 128, 128], P(('atm', 'ocn')), may hold values from -0.3125 to 0.3125
- back_src_dev: int32 [24576, 1], P(('atm', 'ocn')), may hold values from 0 to 127, as said below
- back_src_tile: int32 [24576], P(('atm', 'ocn')), may hold values from 0 to 7
- back_dst_tile: int32 [24576], P(('atm', 'ocn')), may hold values from 0 to 127
Outputs:
- ocean_import: float32 [1024, 24, 128], P(('atm', 'ocn'))
- atm_import: float32 [16384, 24, 128], P(('atm', 'ocn'))
The draws below stay inside these ranges and needn't reach their ends.
Inputs may be any that keep to these rules, and one draw needn't show every extreme that they name: `fwd_dst_dev`: device d has atm index d // 8 and ocn index d % 8; the device named by a block of device b // 192 differs from it by at most one in each index, counted with wrap-around (nine neighbours, itself included). Among the 192 blocks of one device at most 48 name the same device, and on every device exactly one device is named 48 times. `back_src_dev`: device d has atm index d // 8 and ocn index d % 8; the device named by a block of device b // 192 differs from it by at most one in each index, counted with wrap-around (nine neighbours, itself included). Among the 192 blocks of one device at most 48 name the same device, and on every device exactly one device is named 48 times.
All inputs are finite; a program needn't handle non-finite values. No bound on the sum of `wet_mask` on one device may be relied on, other than what follows from the above.
Results may differ from the reference program's by a relative error of at most 0.0022.
Values may be sent and summed in bfloat16 or wider, within the bound.
A program may use at most 128 MiB of HBM per device.

```python
import jax
import jax.numpy as jnp
import numpy as np
from jax import lax

C = 128
F = 24
ATM_DEV = 128
OCN_DEV = 8
BLK_DEV = 192
BLOCKS = 24576
ATM_TILES = 16384
OCEAN_TILES = 1024
N_OCN = 8
DEVICES = 128


def near_owners(key):
    unit = BLK_DEV // 24
    pattern = jnp.asarray(np.repeat(np.repeat(np.arange(9), [6, 5, 4, 3, 2, 1, 1, 1, 1]), unit), dtype=jnp.int32)
    n_atmos = DEVICES // N_OCN

    def one_device(device_key, device):
        first_key, second_key = jax.random.split(device_key)
        shuffle = jax.random.permutation(first_key, 9).astype(jnp.int32)
        chosen = jax.random.permutation(second_key, shuffle[pattern]).astype(jnp.int32)
        row_step = chosen // 3 - 1
        col_step = chosen % 3 - 1
        here_row = device // N_OCN
        here_col = device % N_OCN
        owner = (here_row + row_step) % n_atmos * N_OCN + (here_col + col_step) % N_OCN
        return owner.astype(jnp.int32)
    device_keys = jax.random.split(key, DEVICES)
    owners = jax.vmap(one_device)(device_keys, jnp.arange(DEVICES, dtype=jnp.int32))
    return owners.reshape(BLOCKS, 1).astype(jnp.int32)


def draw_fwd_dst_dev(key, part):
    return near_owners(jax.random.fold_in(key, 11))


def draw_back_src_dev(key, part):
    return near_owners(jax.random.fold_in(key, 23))


def with_ends(entries, rng, low, top_value):
    extent = entries.shape
    place = [jax.random.randint(jax.random.fold_in(rng, axis), (), 0, extent[axis]) for axis in range(len(extent))]
    entries = entries.at[tuple(place)].set(low)
    longest = extent.index(max(extent))
    place[longest] = (place[longest] + 1) % extent[longest]
    return entries.at[tuple(place)].set(top_value)


def levels(own_key, extent, shards, least, high):
    gain, own = 1.0, jax.random.fold_in(own_key, 6)
    for axis_at, blocks in shards:
        steps = jnp.exp(jax.random.uniform(jax.random.fold_in(own, axis_at), (blocks,), jnp.float32, least / len(shards), high / len(shards)))
        gain = gain * jnp.repeat(steps, extent[axis_at] // blocks).reshape([-1 if axis == axis_at else 1 for axis in range(len(extent))])
    return gain


def gaussian(key, extent, width, bound, cuts=(), kind=jnp.bfloat16):
    entries = jax.random.normal(key, extent, jnp.float32) * width
    if len(cuts) > 0:
        entries = levels(key, extent, cuts, -0.22, 0.18) * entries
    return jnp.clip(entries, min=-bound, max=bound).astype(kind)


def setup_inputs(seed: int = 0) -> dict:
    seeds = jax.random.split(jax.random.key(seed), 12)
    return {
        "atm_fields": gaussian(seeds[0], (ATM_TILES, F, C), 1.0, 6.0, ((0, 128),)),
        "fwd_blocks": gaussian(seeds[1], (BLOCKS, C, C), (6 * C) ** -0.5, 0.21875, ((0, 128),)),
        "fwd_src_tile": with_ends(jax.random.randint(seeds[2], (BLOCKS,), 0, ATM_DEV), jax.random.fold_in(seeds[2], 1), 0, ATM_DEV - 1).astype(jnp.int32),
        "fwd_dst_dev": draw_fwd_dst_dev(jax.random.fold_in(seeds[11], 71), 0),
        "fwd_dst_tile": with_ends(jax.random.randint(seeds[4], (BLOCKS,), 0, OCN_DEV), jax.random.fold_in(seeds[4], 1), 0, OCN_DEV - 1).astype(jnp.int32),
        "ocean_state": gaussian(seeds[5], (OCEAN_TILES, F, C), 1.0, 6.0, ((0, 128),), jnp.float32),
        "wet_mask": with_ends((jax.random.randint(seeds[6], (OCEAN_TILES, C), 0, 4) < 3).astype(jnp.int32), jax.random.fold_in(seeds[6], 1), 0, 1),
        "back_blocks": gaussian(seeds[7], (BLOCKS, C, C), (3 * C) ** -0.5, 0.3125, ((0, 128),)),
        "back_src_dev": draw_back_src_dev(jax.random.fold_in(seeds[11], 71), 0),
        "back_src_tile": with_ends(jax.random.randint(seeds[9], (BLOCKS,), 0, OCN_DEV), jax.random.fold_in(seeds[9], 1), 0, OCN_DEV - 1).astype(jnp.int32),
        "back_dst_tile": with_ends(jax.random.randint(seeds[10], (BLOCKS,), 0, ATM_DEV), jax.random.fold_in(seeds[10], 1), 0, ATM_DEV - 1).astype(jnp.int32),
    }


def block_products(sources, weights):
    def one(pair):
        left, right = pair
        return jnp.einsum("bfi,bij->bfj", left.astype(jnp.float32), right.astype(jnp.float32))
    return lax.map(one, (sources.reshape(DEVICES, BLK_DEV, F, C), weights.reshape(DEVICES, BLK_DEV, C, C))).reshape(BLOCKS, F, C)


def reference(atm_fields, fwd_blocks, fwd_src_tile, fwd_dst_dev, fwd_dst_tile, ocean_state, wet_mask, back_blocks, back_src_dev, back_src_tile, back_dst_tile):
    owner_dev = (jnp.arange(BLOCKS, dtype=jnp.int32) // BLK_DEV).astype(jnp.int32)
    source_rows = (owner_dev * ATM_DEV + fwd_src_tile).astype(jnp.int32)
    fwd_part = block_products(atm_fields[source_rows], fwd_blocks)
    target_rows = (fwd_dst_dev[:, 0] * OCN_DEV + fwd_dst_tile).astype(jnp.int32)
    ocean_import = jax.ops.segment_sum(fwd_part, target_rows, num_segments=OCEAN_TILES)
    wet = wet_mask.astype(jnp.float32)[:, None, :]
    response = (wet * jnp.tanh(ocean_state + ocean_import)).astype(jnp.bfloat16)
    ocean_rows = (back_src_dev[:, 0] * OCN_DEV + back_src_tile).astype(jnp.int32)
    back_part = block_products(response[ocean_rows], back_blocks)
    atm_rows = (owner_dev * ATM_DEV + back_dst_tile).astype(jnp.int32)
    atm_import = jax.ops.segment_sum(back_part, atm_rows, num_segments=ATM_TILES)
    return ocean_import, atm_import
```

```python
import functools

import jax
import jax.numpy as jnp
from jax import lax
from jax.experimental import pallas as pl
from jax.experimental.pallas import tpu as pltpu
from jax.sharding import PartitionSpec as P

MESH = pl.DeviceIdType.MESH
I32 = jnp.int32
F32 = jnp.float32
HALVES = 2
LEVELS = 32766.0
ORDER = (0, 2, 6, 8, 1, 7, 3, 5)
SELF = 4


def steps(n):
    return n // 3 - 1, n % 3 - 1


def neighbour_keys(dev, tile, here_row, here_col, n_row, n_col, tiles):
    shift = n_col.bit_length() - 1
    rel_row = ((dev >> shift) - here_row) & (n_row - 1)
    rel_col = ((dev & (n_col - 1)) - here_col) & (n_col - 1)
    row_step = jnp.where(rel_row == n_row - 1, 0, jnp.where(rel_row == 0, 1, 2))
    col_step = jnp.where(rel_col == n_col - 1, 0, jnp.where(rel_col == 0, 1, 2))
    return (row_step * 3 + col_step) * tiles + tile


def sorted_order(key, src, tiles):
    count = key.shape[1]
    group = count // HALVES
    lane = lax.broadcasted_iota(I32, (1, count), 1)
    half = jnp.zeros_like(lane)
    for h in range(1, HALVES):
        half = half + (lane >= h * group).astype(I32)
    wide_key = half * 128 + key
    rank_row = wide_key * 256 + lane
    eye = lax.broadcasted_iota(I32, (count, count), 0) == lax.broadcasted_iota(
        I32, (count, count), 1
    )

    def column(row):
        return jnp.sum(jnp.where(eye, row, 0), axis=1, keepdims=True)

    rank_col = column(rank_row)
    src_col = column(src)
    place = jnp.sum((rank_row < rank_col).astype(I32), axis=1, keepdims=True)
    lanes = lax.broadcasted_iota(I32, (count, 256), 1)
    hit = place == lanes
    local = (rank_col & 255) - (rank_col >> 15) * group
    key_col = rank_col >> 8

    def arranged(col):
        return jnp.sum(jnp.where(hit, col, 0), axis=0, keepdims=True)

    rows = [arranged(local), arranged(src_col), arranged(key_col)]
    for h in range(HALVES):
        slot = lanes + h * 128
        inside = (key_col == slot) & (lanes < 128)
        upto = jnp.sum((key_col <= slot).astype(I32), axis=0, keepdims=True)
        some = jnp.sum(inside.astype(I32), axis=0, keepdims=True)
        rows.append(jnp.where(some > 0, upto - 1, -1))
    return rows


def exchange(
    n_row,
    n_col,
    src_hbm,
    dev_hbm,
    tile_hbm,
    atm_hbm,
    w_hbm,
    state_hbm,
    mask_hbm,
    import_ref,
    near_ref,
    src_ref,
    dev_ref,
    tile_ref,
    state_ref,
    mask_ref,
    small_sem,
    atm_v,
    *scratch,
):
    w_v = scratch[:HALVES]
    (
        sums,
        prep_v,
        prep_s,
        q_out,
        scale_out,
        q_in,
        scale_in,
        atm_sem,
        w_sem,
        prep_sem,
        send_sem,
        recv_sem,
        scale_send_sem,
        scale_recv_sem,
        resp_send_sem,
        resp_recv_sem,
    ) = scratch[HALVES:]
    count = dev_ref.shape[1]
    group = count // HALVES
    tiles, fields, cells = state_ref.shape
    row = lax.axis_index("atm")
    col = lax.axis_index("ocn")

    def device(n):
        dr, dc = steps(n)
        return (lax.rem(row + dr + n_row, n_row), lax.rem(col + dc + n_col, n_col))

    barrier = pltpu.get_barrier_semaphore()
    for n in ORDER:
        pl.semaphore_signal(barrier, inc=1, device_id=device(n), device_id_type=MESH)

    small_copies = [
        pltpu.make_async_copy(source, target, small_sem.at[i])
        for i, (source, target) in enumerate(
            (
                (src_hbm, src_ref),
                (dev_hbm, dev_ref),
                (tile_hbm, tile_ref),
                (state_hbm, state_ref),
                (mask_hbm, mask_ref),
            )
        )
    ]
    for copy in small_copies:
        copy.start()
    atm_copy = pltpu.make_async_copy(atm_hbm, atm_v, atm_sem)
    atm_copy.start()
    w_copies = []
    for h in range(HALVES):
        copy = pltpu.make_async_copy(
            w_hbm.at[pl.ds(h * group, group)], w_v[h], w_sem.at[h]
        )
        copy.start()
        w_copies.append(copy)

    for copy in small_copies[:3]:
        copy.wait()
    key = neighbour_keys(dev_ref[...], tile_ref[...], row, col, n_row, n_col, tiles)
    rows = sorted_order(key, src_ref[...], tiles)
    for i, values in enumerate(rows):
        prep_v[i : i + 1, :] = values
    prep_copy = pltpu.make_async_copy(prep_v, prep_s, prep_sem)
    prep_copy.start()
    prep_copy.wait()
    atm_copy.wait()

    for h in range(HALVES):
        w_copies[h].wait()

        def one(i, total, h=h):
            k = h * group + i
            before = prep_s[2, jnp.maximum(k - 1, 0)]
            keep = jnp.where((prep_s[2, k] == before) & (i > 0), 1.0, 0.0).astype(F32)
            product = jnp.dot(
                atm_v[prep_s[1, k]], w_v[h][prep_s[0, k]], preferred_element_type=F32
            )
            total = total * keep + product
            sums[k] = total
            return total

        lax.fori_loop(0, group, one, jnp.zeros((fields, cells), F32), unroll=8)

    def slot_sum(slot):
        total = None
        for h in range(HALVES):
            last = prep_s[3 + h, slot]
            part = sums[jnp.maximum(last, 0)] * jnp.where(last >= 0, 1.0, 0.0).astype(F32)
            total = part if total is None else total + part
        return total

    pl.semaphore_wait(barrier, 8)
    copies = []
    for n in ORDER:
        for t in range(tiles):
            total = slot_sum(n * tiles + t)
            top = jnp.max(jnp.abs(total), axis=0, keepdims=True)
            q_out[n, t] = jnp.round(total * (LEVELS / jnp.maximum(top, 1e-30))).astype(
                jnp.int16
            )
            scale_out[n, t : t + 1] = top * (1.0 / LEVELS)
        for out, land, s_sem, r_sem in (
            (q_out, q_in, send_sem, recv_sem),
            (scale_out, scale_in, scale_send_sem, scale_recv_sem),
        ):
            copy = pltpu.make_async_remote_copy(
                src_ref=out.at[n],
                dst_ref=land.at[8 - n],
                send_sem=s_sem.at[n],
                recv_sem=r_sem.at[8 - n],
                device_id=device(n),
                device_id_type=MESH,
            )
            copy.start()
            copies.append(copy)
    for t in range(tiles):
        import_ref[t] = slot_sum(SELF * tiles + t)
    for copy in small_copies[3:]:
        copy.wait()
    for copy in copies:
        copy.wait()

    for t in range(tiles):
        total = import_ref[t]
        for n in ORDER:
            total = total + q_in[n, t].astype(F32) * scale_in[n, t : t + 1]
        import_ref[t] = total
        wet = mask_ref[t : t + 1].astype(F32)
        near_ref[SELF, t] = (wet * jnp.tanh(state_ref[t] + total)).astype(jnp.bfloat16)

    copies = []
    for n in ORDER:
        copy = pltpu.make_async_remote_copy(
            src_ref=near_ref.at[SELF],
            dst_ref=near_ref.at[8 - n],
            send_sem=resp_send_sem.at[n],
            recv_sem=resp_recv_sem.at[8 - n],
            device_id=device(n),
            device_id_type=MESH,
        )
        copy.start()
        copies.append(copy)
    for copy in copies:
        copy.wait()


def backward(n_row, n_col, dev_ref, tile_ref, dst_ref, near_ref, import_ref, w_ref, imported_ref, out_ref):
    count = dst_ref.shape[0]
    atmos, fields, cells = out_ref.shape
    tiles = near_ref.shape[0] // 9
    row = lax.axis_index("atm")
    col = lax.axis_index("ocn")
    imported_ref[...] = import_ref[...]

    def clear(t, _):
        out_ref[t] = jnp.zeros((fields, cells), F32)
        return 0

    lax.fori_loop(0, atmos, clear, 0, unroll=8)

    def one(b, _):
        slot = neighbour_keys(dev_ref[b], tile_ref[b], row, col, n_row, n_col, tiles)
        product = jnp.dot(near_ref[slot], w_ref[b], preferred_element_type=F32)
        dst = dst_ref[b]
        out_ref[dst] = out_ref[dst] + product
        return 0

    lax.fori_loop(0, count, one, 0, unroll=8)


def shards(
    atm_fields,
    fwd_blocks,
    fwd_src_tile,
    fwd_dst_dev,
    fwd_dst_tile,
    ocean_state,
    wet_mask,
    back_blocks,
    back_src_dev,
    back_src_tile,
    back_dst_tile,
):
    n_row = lax.axis_size("atm")
    n_col = lax.axis_size("ocn")
    blocks, cells, _ = fwd_blocks.shape
    group = blocks // HALVES
    atmos, fields, _ = atm_fields.shape
    tiles = ocean_state.shape[0]
    vmem = pl.BlockSpec(memory_space=pltpu.VMEM)
    smem = pl.BlockSpec(memory_space=pltpu.SMEM)
    hbm = pl.BlockSpec(memory_space=pltpu.HBM)
    ocean_import, near = pl.pallas_call(
        functools.partial(exchange, n_row, n_col),
        out_shape=(
            jax.ShapeDtypeStruct((tiles, fields, cells), F32),
            jax.ShapeDtypeStruct((9, tiles, fields, cells), jnp.bfloat16),
        ),
        in_specs=[hbm] * 7,
        out_specs=(vmem, vmem),
        scratch_shapes=[
            pltpu.VMEM((1, blocks), I32),
            pltpu.VMEM((1, blocks), I32),
            pltpu.VMEM((1, blocks), I32),
            pltpu.VMEM((tiles, fields, cells), F32),
            pltpu.VMEM((tiles, cells), I32),
            pltpu.SemaphoreType.DMA((5,)),
            pltpu.VMEM((atmos, fields, cells), jnp.bfloat16),
            *[pltpu.VMEM((group, cells, cells), jnp.bfloat16)] * HALVES,
            pltpu.VMEM((blocks, fields, cells), F32),
            pltpu.VMEM((8, 256), I32),
            pltpu.SMEM((8, 256), I32),
            pltpu.VMEM((9, tiles, fields, cells), jnp.int16),
            pltpu.VMEM((9, tiles, cells), F32),
            pltpu.VMEM((9, tiles, fields, cells), jnp.int16),
            pltpu.VMEM((9, tiles, cells), F32),
            pltpu.SemaphoreType.DMA,
            pltpu.SemaphoreType.DMA((HALVES,)),
            pltpu.SemaphoreType.DMA,
            *[pltpu.SemaphoreType.DMA((9,))] * 6,
        ],
        compiler_params=pltpu.CompilerParams(
            collective_id=0, has_side_effects=True, vmem_limit_bytes=24 * 2**20
        ),
        name="exchange",
    )(
        *[
            pltpu.with_memory_space_constraint(operand, pltpu.HBM)
            for operand in (
                fwd_src_tile.reshape(1, blocks),
                fwd_dst_dev.reshape(1, blocks),
                fwd_dst_tile.reshape(1, blocks),
                atm_fields,
                fwd_blocks,
                ocean_state,
                wet_mask,
            )
        ]
    )
    return pl.pallas_call(
        functools.partial(backward, n_row, n_col),
        out_shape=(
            jax.ShapeDtypeStruct((tiles, fields, cells), F32),
            jax.ShapeDtypeStruct((atmos, fields, cells), F32),
        ),
        in_specs=[smem, smem, smem, vmem, vmem, vmem],
        out_specs=(vmem, vmem),
        compiler_params=pltpu.CompilerParams(vmem_limit_bytes=24 * 2**20),
        name="backward",
    )(
        back_src_dev.reshape(blocks),
        back_src_tile,
        back_dst_tile,
        near.reshape(9 * tiles, fields, cells),
        ocean_import,
        back_blocks,
    )


def solution(mesh):
    both = ("atm", "ocn")
    in_specs = (
        P(both, None, None),
        P(both, None, None),
        P(both),
        P(both, None),
        P(both),
        P(both, None, None),
        P(both, None),
        P(both, None, None),
        P(both, None),
        P(both),
        P(both),
    )
    out_specs = (P(both, None, None), P(both, None, None))
    return jax.shard_map(shards, mesh=mesh, in_specs=in_specs, out_specs=out_specs, check_vma=False)
```

```python
import functools

import jax
import jax.numpy as jnp
from jax import lax
from jax.experimental import pallas as pl
from jax.experimental.pallas import tpu as pltpu
from jax.sharding import PartitionSpec as P

MESH = pl.DeviceIdType.MESH
I32 = jnp.int32
F32 = jnp.float32
HALVES = 2
PARTS = 2
LEVELS = 32000.0
LOG2_E = 1.4426950408889634
EARLY = 8
PREP_ROWS = 8
ORDER = (0, 2, 6, 8, 1, 7, 3, 5)
SELF = 4


def steps(n):
    return n // 3 - 1, n % 3 - 1


def neighbour_keys(dev, tile, here_row, here_col, n_row, n_col, tiles):
    shift = n_col.bit_length() - 1
    rel_row = ((dev >> shift) - here_row) & (n_row - 1)
    rel_col = ((dev & (n_col - 1)) - here_col) & (n_col - 1)
    row_step = jnp.where(rel_row == n_row - 1, 0, jnp.where(rel_row == 0, 1, 2))
    col_step = jnp.where(rel_col == n_col - 1, 0, jnp.where(rel_col == 0, 1, 2))
    return (row_step * 3 + col_step) * tiles + tile


def sorted_order(key, src, tiles):
    count = key.shape[1]
    group = count // HALVES
    lane = lax.broadcasted_iota(I32, (1, count), 1)
    half = jnp.zeros_like(lane)
    for h in range(1, HALVES):
        half = half + (lane >= h * group).astype(I32)
    wide_key = half * 128 + key
    rank_row = wide_key * 256 + lane
    eye = lax.broadcasted_iota(I32, (count, count), 0) == lax.broadcasted_iota(
        I32, (count, count), 1
    )

    def column(row):
        return jnp.sum(jnp.where(eye, row, 0), axis=1, keepdims=True)

    rank_col = column(rank_row)
    src_col = column(src)
    place = jnp.sum((rank_row < rank_col).astype(I32), axis=1, keepdims=True)
    lanes = lax.broadcasted_iota(I32, (count, 256), 1)
    hit = place == lanes
    local = (rank_col & 255) - (rank_col >> 15) * group
    key_col = rank_col >> 8

    def arranged(col):
        return jnp.sum(jnp.where(hit, col, 0), axis=0, keepdims=True)

    rows = [arranged(local), arranged(src_col), arranged(key_col)]
    for h in range(HALVES):
        slot = lanes + h * 128
        inside = (key_col == slot) & (lanes < 128)
        upto = jnp.sum((key_col <= slot).astype(I32), axis=0, keepdims=True)
        some = jnp.sum(inside.astype(I32), axis=0, keepdims=True)
        rows.append(jnp.where(some > 0, upto - 1, -1))
    return rows


def pair_products(left, right):
    rows, cols = left[0].shape[0], right[0].shape[1]
    product = jnp.dot(
        jnp.concatenate(left, axis=0),
        jnp.concatenate(right, axis=1),
        preferred_element_type=F32,
    )
    return product[:rows, :cols], product[rows:, cols:]


def exchange(
    n_row,
    n_col,
    src_hbm,
    dev_hbm,
    tile_hbm,
    atm_hbm,
    w_hbm,
    state_hbm,
    mask_hbm,
    back_hbm,
    back_dev_hbm,
    back_tile_hbm,
    back_dst_hbm,
    import_ref,
    near_ref,
    back_ref,
    order_ref,
    src_ref,
    dev_ref,
    tile_ref,
    back_order,
    state_ref,
    mask_ref,
    small_sem,
    order_sem,
    back_sem,
    atm_v,
    *scratch,
):
    w_v = scratch[:HALVES]
    (
        sums,
        prep_v,
        prep_s,
        q_out,
            q_in,
        atm_sem,
        w_sem,
        prep_sem,
        send_sem,
        recv_sem,
        resp_send_sem,
        resp_recv_sem,
    ) = scratch[HALVES:]
    count = dev_ref.shape[1]
    group = count // HALVES
    tiles, fields, cells = state_ref.shape
    row = lax.axis_index("atm")
    col = lax.axis_index("ocn")

    def device(n):
        dr, dc = steps(n)
        return (lax.rem(row + dr + n_row, n_row), lax.rem(col + dc + n_col, n_col))

    def w_copy(h):
        return pltpu.make_async_copy(
            w_hbm.at[pl.ds(h * group, group)], w_v[h], w_sem.at[h]
        )

    w_copy(0).start()
    barrier = pltpu.get_barrier_semaphore()
    for n in ORDER:
        pl.semaphore_signal(barrier, inc=1, device_id=device(n), device_id_type=MESH)

    small_copies = [
        pltpu.make_async_copy(source, target, small_sem.at[i])
        for i, (source, target) in enumerate(
            (
                (src_hbm, src_ref),
                (dev_hbm, dev_ref),
                (tile_hbm, tile_ref),
                (state_hbm, state_ref),
                (mask_hbm, mask_ref),
                (back_dev_hbm, back_order.at[pl.ds(0, 1)]),
                (back_tile_hbm, back_order.at[pl.ds(1, 1)]),
                (back_dst_hbm, back_order.at[pl.ds(2, 1)]),
            )
        )
    ]
    for copy in small_copies[:3]:
        copy.start()
    atm_copy = pltpu.make_async_copy(atm_hbm, atm_v, atm_sem)
    atm_copy.start()
    for copy in small_copies[:3]:
        copy.wait()
    key = neighbour_keys(dev_ref[...], tile_ref[...], row, col, n_row, n_col, tiles)
    rows = sorted_order(key, src_ref[...], tiles)
    for i, values in enumerate(rows):
        prep_v[i : i + 1, :] = values
    prep_copy = pltpu.make_async_copy(prep_v, prep_s, prep_sem)
    prep_copy.start()
    for h in range(1, HALVES):
        w_copy(h).start()
    for copy in small_copies[3:]:
        copy.start()
    prep_copy.wait()
    atm_copy.wait()

    back_copy = pltpu.make_async_copy(back_hbm, back_ref, back_sem)
    for h in range(HALVES):
        w_copy(h).wait()

        def two(i, total, h=h):
            k = h * group + 2 * i
            products = pair_products(
                [atm_v[prep_s[1, k + side]] for side in range(2)],
                [w_v[h][prep_s[0, k + side]] for side in range(2)],
            )
            for side in range(2):
                before = prep_s[2, jnp.maximum(k + side - 1, 0)]
                same = (prep_s[2, k + side] == before) & (2 * i + side > 0)
                keep = jnp.where(same, 1.0, 0.0).astype(F32)
                total = total * keep + products[side]
                sums[k + side] = total
            return total

        lax.fori_loop(
            0, group // 2, two, jnp.zeros((fields, cells), F32), unroll=group // 2
        )

    def slot_sum(slot):
        total = None
        for h in range(HALVES):
            last = prep_s[3 + h, slot]
            part = sums[jnp.maximum(last, 0)] * jnp.where(last >= 0, 1.0, 0.0).astype(F32)
            total = part if total is None else total + part
        return total

    part = tiles // PARTS
    pair = part // 2
    values = pair * fields
    used = pl.ds(0, values + part)

    def encode(n, c):
        exponents = []
        levels = []
        for i in range(part):
            total = slot_sum(n * tiles + c * part + i)
            top = jnp.maximum(jnp.max(jnp.abs(total), axis=0, keepdims=True), 1e-30)
            exponent = jnp.ceil(jnp.log(top * (1.0 / LEVELS)) * LOG2_E)
            levels.append(jnp.round(total * jnp.exp2(-exponent)).astype(I32))
            exponents.append(exponent.astype(I32))
        for i in range(pair):
            packed = (levels[i] << 16) | (levels[i + pair] & 0xFFFF)
            q_out[c, n, i * fields : (i + 1) * fields] = packed
        for i in range(part):
            q_out[c, n, values + i : values + i + 1] = exponents[i]

    arriving = []

    def send(n, c):
        copy = pltpu.make_async_remote_copy(
            src_ref=q_out.at[c, n, used],
            dst_ref=q_in.at[c, 8 - n, used],
            send_sem=send_sem.at[c, n],
            recv_sem=recv_sem.at[c, 8 - n],
            device_id=device(n),
            device_id_type=MESH,
        )
        copy.start()
        arriving[c].append(copy)

    for n in ORDER[:EARLY]:
        encode(n, 0)
    pl.semaphore_wait(barrier, 8)
    for c in range(PARTS):
        arriving.append([])
        for i, n in enumerate(ORDER):
            if c > 0 or i >= EARLY:
                encode(n, c)
            send(n, c)
    back_copy.start()
    for t in range(tiles):
        import_ref[t] = slot_sum(SELF * tiles + t)
    for copy in small_copies[3:]:
        copy.wait()
    back_order[0:1] = neighbour_keys(
        back_order[0:1], back_order[1:2], row, col, n_row, n_col, tiles
    )
    order_copy = pltpu.make_async_copy(back_order, order_ref, order_sem)
    order_copy.start()

    answers = []
    for c in range(PARTS):
        span = pl.ds(c * part, part)
        for copy in arriving[c]:
            copy.wait_recv()
        for i in range(part):
            t = c * part + i
            total = import_ref[t]
            for n in ORDER:
                packed = q_in[c, n, (i % pair) * fields : (i % pair + 1) * fields]
                level = packed >> 16 if i < pair else (packed << 16) >> 16
                exponent = q_in[c, n, values + i : values + i + 1].astype(F32)
                total = total + level.astype(F32) * jnp.exp2(exponent)
            import_ref[t] = total
            wet = mask_ref[t : t + 1].astype(F32)
            near_ref[SELF, t] = (wet * jnp.tanh(state_ref[t] + total)).astype(jnp.bfloat16)
        for n in ORDER:
            copy = pltpu.make_async_remote_copy(
                src_ref=near_ref.at[SELF, span],
                dst_ref=near_ref.at[8 - n, span],
                send_sem=resp_send_sem.at[c, n],
                recv_sem=resp_recv_sem.at[c, 8 - n],
                device_id=device(n),
                device_id_type=MESH,
            )
            copy.start()
            answers.append(copy)
    back_copy.wait()
    order_copy.wait()
    for copies in arriving:
        for copy in copies:
            copy.wait_send()
    for copy in answers:
        copy.wait()


def backward(order_ref, near_ref, import_ref, w_ref, imported_ref, out_ref):
    count = order_ref.shape[1]
    atmos, fields, cells = out_ref.shape
    imported_ref[...] = import_ref[...]

    def clear(t, _):
        out_ref[t] = jnp.zeros((fields, cells), F32)
        return 0

    lax.fori_loop(0, atmos, clear, 0, unroll=atmos)

    def two(i, _):
        b = 2 * i
        products = pair_products(
            [near_ref[order_ref[0, b + side]] for side in range(2)],
            [w_ref[b + side] for side in range(2)],
        )
        for side in range(2):
            dst = order_ref[2, b + side]
            out_ref[dst] = out_ref[dst] + products[side]
        return 0

    lax.fori_loop(0, count // 2, two, 0, unroll=count // 2)


def shards(
    atm_fields,
    fwd_blocks,
    fwd_src_tile,
    fwd_dst_dev,
    fwd_dst_tile,
    ocean_state,
    wet_mask,
    back_blocks,
    back_src_dev,
    back_src_tile,
    back_dst_tile,
):
    n_row = lax.axis_size("atm")
    n_col = lax.axis_size("ocn")
    blocks, cells, _ = fwd_blocks.shape
    group = blocks // HALVES
    atmos, fields, _ = atm_fields.shape
    tiles = ocean_state.shape[0]
    rows = tiles // PARTS // 2 * fields + 8
    vmem = pl.BlockSpec(memory_space=pltpu.VMEM)
    smem = pl.BlockSpec(memory_space=pltpu.SMEM)
    hbm = pl.BlockSpec(memory_space=pltpu.HBM)
    ocean_import, near, back_near, order = pl.pallas_call(
        functools.partial(exchange, n_row, n_col),
        out_shape=(
            jax.ShapeDtypeStruct((tiles, fields, cells), F32),
            jax.ShapeDtypeStruct((9, tiles, fields, cells), jnp.bfloat16),
            jax.ShapeDtypeStruct((blocks, cells, cells), jnp.bfloat16),
            pltpu.SMEM((3, blocks), I32),
        ),
        in_specs=[hbm] * 11,
        out_specs=(vmem, vmem, vmem, smem),
        scratch_shapes=[
            pltpu.VMEM((1, blocks), I32),
            pltpu.VMEM((1, blocks), I32),
            pltpu.VMEM((1, blocks), I32),
            pltpu.VMEM((3, blocks), I32),
            pltpu.VMEM((tiles, fields, cells), F32),
            pltpu.VMEM((tiles, cells), I32),
            pltpu.SemaphoreType.DMA((8,)),
            pltpu.SemaphoreType.DMA,
            pltpu.SemaphoreType.DMA,
            pltpu.VMEM((atmos, fields, cells), jnp.bfloat16),
            *[pltpu.VMEM((group, cells, cells), jnp.bfloat16)] * HALVES,
            pltpu.VMEM((blocks, fields, cells), F32),
            pltpu.VMEM((PREP_ROWS, 256), I32),
            pltpu.SMEM((PREP_ROWS, 256), I32),
            pltpu.VMEM((PARTS, 9, rows, cells), I32),
            pltpu.VMEM((PARTS, 9, rows, cells), I32),
            pltpu.SemaphoreType.DMA,
            pltpu.SemaphoreType.DMA((HALVES,)),
            pltpu.SemaphoreType.DMA,
            *[pltpu.SemaphoreType.DMA((PARTS, 9))] * 4,
        ],
        compiler_params=pltpu.CompilerParams(
            collective_id=0, has_side_effects=True, vmem_limit_bytes=28 * 2**20
        ),
        name="exchange",
    )(
        *[
            pltpu.with_memory_space_constraint(operand, pltpu.HBM)
            for operand in (
                fwd_src_tile.reshape(1, blocks),
                fwd_dst_dev.reshape(1, blocks),
                fwd_dst_tile.reshape(1, blocks),
                atm_fields,
                fwd_blocks,
                ocean_state,
                wet_mask,
                back_blocks,
                back_src_dev.reshape(1, blocks),
                back_src_tile.reshape(1, blocks),
                back_dst_tile.reshape(1, blocks),
            )
        ]
    )
    return pl.pallas_call(
        backward,
        out_shape=(
            jax.ShapeDtypeStruct((tiles, fields, cells), F32),
            jax.ShapeDtypeStruct((atmos, fields, cells), F32),
        ),
        in_specs=[smem, vmem, vmem, vmem],
        out_specs=(vmem, vmem),
        compiler_params=pltpu.CompilerParams(vmem_limit_bytes=28 * 2**20),
        name="backward",
    )(
        pltpu.with_memory_space_constraint(order, pltpu.SMEM),
        near.reshape(9 * tiles, fields, cells),
        ocean_import,
        back_near,
    )


def solution(mesh):
    both = ("atm", "ocn")
    in_specs = (
        P(both, None, None),
        P(both, None, None),
        P(both),
        P(both, None),
        P(both),
        P(both, None, None),
        P(both, None),
        P(both, None, None),
        P(both, None),
        P(both),
        P(both),
    )
    out_specs = (P(both, None, None), P(both, None, None))
    return jax.shard_map(shards, mesh=mesh, in_specs=in_specs, out_specs=out_specs, check_vma=False)
```

```python
import functools

import jax
import jax.numpy as jnp
from jax import lax
from jax.experimental import pallas as pl
from jax.experimental.pallas import tpu as pltpu
from jax.sharding import PartitionSpec as P

MESH = pl.DeviceIdType.MESH
I32 = jnp.int32
F32 = jnp.float32
HALVES = 2
PARTS = 2
LEVELS = 32000.0
LOG2_E = 1.4426950408889634
PREP_ROWS = 8
ORDER = (0, 2, 6, 8, 1, 7, 3, 5)
SELF = 4


def steps(n):
    return n // 3 - 1, n % 3 - 1


def neighbour_keys(dev, tile, here_row, here_col, n_row, n_col, tiles):
    shift = n_col.bit_length() - 1
    rel_row = ((dev >> shift) - here_row) & (n_row - 1)
    rel_col = ((dev & (n_col - 1)) - here_col) & (n_col - 1)
    row_step = jnp.where(rel_row == n_row - 1, 0, jnp.where(rel_row == 0, 1, 2))
    col_step = jnp.where(rel_col == n_col - 1, 0, jnp.where(rel_col == 0, 1, 2))
    return (row_step * 3 + col_step) * tiles + tile


def sorted_order(key, src, tiles):
    count = key.shape[1]
    group = count // HALVES
    lane = lax.broadcasted_iota(I32, (1, count), 1)
    half = jnp.zeros_like(lane)
    for h in range(1, HALVES):
        half = half + (lane >= h * group).astype(I32)
    wide_key = half * 128 + key
    rank_row = wide_key * 256 + lane
    eye = lax.broadcasted_iota(I32, (count, count), 0) == lax.broadcasted_iota(
        I32, (count, count), 1
    )

    def column(row):
        return jnp.sum(jnp.where(eye, row, 0), axis=1, keepdims=True)

    rank_col = column(rank_row)
    src_col = column(src)
    place = jnp.sum((rank_row < rank_col).astype(I32), axis=1, keepdims=True)
    lanes = lax.broadcasted_iota(I32, (count, 256), 1)
    hit = place == lanes
    local = (rank_col & 255) - (rank_col >> 15) * group
    key_col = rank_col >> 8

    def arranged(col):
        return jnp.sum(jnp.where(hit, col, 0), axis=0, keepdims=True)

    rows = [arranged(local), arranged(src_col), arranged(key_col)]
    for h in range(HALVES):
        slot = lanes + h * 128
        inside = (key_col == slot) & (lanes < 128)
        upto = jnp.sum((key_col <= slot).astype(I32), axis=0, keepdims=True)
        some = jnp.sum(inside.astype(I32), axis=0, keepdims=True)
        rows.append(jnp.where(some > 0, upto - 1, -1))
    return rows


def pair_products(left, right):
    rows, cols = left[0].shape[0], right[0].shape[1]
    product = jnp.dot(
        jnp.concatenate(left, axis=0),
        jnp.concatenate(right, axis=1),
        preferred_element_type=F32,
    )
    return product[:rows, :cols], product[rows:, cols:]


def exchange(
    n_row,
    n_col,
    src_hbm,
    dev_hbm,
    tile_hbm,
    atm_hbm,
    w_hbm,
    state_hbm,
    mask_hbm,
    back_hbm,
    back_dev_hbm,
    back_tile_hbm,
    back_dst_hbm,
    import_ref,
    near_ref,
    back_ref,
    order_ref,
    src_ref,
    dev_ref,
    tile_ref,
    back_order,
    state_ref,
    mask_ref,
    small_sem,
    order_sem,
    back_sem,
    atm_v,
    *scratch,
):
    w_v = scratch[:HALVES]
    (
        sums,
        prep_v,
        prep_s,
        q_out,
            q_in,
        atm_sem,
        w_sem,
        prep_sem,
        send_sem,
        recv_sem,
        resp_send_sem,
        resp_recv_sem,
    ) = scratch[HALVES:]
    count = dev_ref.shape[1]
    group = count // HALVES
    tiles, fields, cells = state_ref.shape
    row = lax.axis_index("atm")
    col = lax.axis_index("ocn")

    def device(n):
        dr, dc = steps(n)
        return (lax.rem(row + dr + n_row, n_row), lax.rem(col + dc + n_col, n_col))

    def w_copy(h):
        return pltpu.make_async_copy(
            w_hbm.at[pl.ds(h * group, group)], w_v[h], w_sem.at[h]
        )

    barrier = pltpu.get_barrier_semaphore()
    for n in ORDER:
        pl.semaphore_signal(barrier, inc=1, device_id=device(n), device_id_type=MESH)

    w_copy(0).start()
    small_copies = [
        pltpu.make_async_copy(source, target, small_sem.at[i])
        for i, (source, target) in enumerate(
            (
                (src_hbm, src_ref),
                (dev_hbm, dev_ref),
                (tile_hbm, tile_ref),
                (state_hbm, state_ref),
                (mask_hbm, mask_ref),
                (back_dev_hbm, back_order.at[pl.ds(0, 1)]),
                (back_tile_hbm, back_order.at[pl.ds(1, 1)]),
                (back_dst_hbm, back_order.at[pl.ds(2, 1)]),
            )
        )
    ]
    for copy in small_copies[:3]:
        copy.start()
    atm_copy = pltpu.make_async_copy(atm_hbm, atm_v, atm_sem)
    atm_copy.start()
    for copy in small_copies[:3]:
        copy.wait()
    key = neighbour_keys(dev_ref[...], tile_ref[...], row, col, n_row, n_col, tiles)
    rows = sorted_order(key, src_ref[...], tiles)
    for i, values in enumerate(rows):
        prep_v[i : i + 1, :] = values
    prep_copy = pltpu.make_async_copy(prep_v, prep_s, prep_sem)
    prep_copy.start()
    for h in range(1, HALVES):
        w_copy(h).start()
    for copy in small_copies[3:]:
        copy.start()
    prep_copy.wait()
    atm_copy.wait()

    back_copy = pltpu.make_async_copy(back_hbm, back_ref, back_sem)
    for h in range(HALVES):
        w_copy(h).wait()

        def two(i, total, h=h):
            k = h * group + 2 * i
            products = pair_products(
                [atm_v[prep_s[1, k + side]] for side in range(2)],
                [w_v[h][prep_s[0, k + side]] for side in range(2)],
            )
            for side in range(2):
                before = prep_s[2, jnp.maximum(k + side - 1, 0)]
                same = (prep_s[2, k + side] == before) & (2 * i + side > 0)
                keep = jnp.where(same, 1.0, 0.0).astype(F32)
                total = total * keep + products[side]
                sums[k + side] = total
            return total

        lax.fori_loop(
            0, group // 2, two, jnp.zeros((fields, cells), F32), unroll=group // 2
        )

    def slot_sum(slot):
        total = None
        for h in range(HALVES):
            last = prep_s[3 + h, slot]
            part = sums[jnp.maximum(last, 0)] * jnp.where(last >= 0, 1.0, 0.0).astype(F32)
            total = part if total is None else total + part
        return total

    part = tiles // PARTS
    pair = part // 2
    values = pair * fields
    used = pl.ds(0, values + part)

    def encode(n, c):
        exponents = []
        levels = []
        for i in range(part):
            total = slot_sum(n * tiles + c * part + i)
            top = jnp.maximum(jnp.max(jnp.abs(total), axis=0, keepdims=True), 1e-30)
            exponent = jnp.ceil(jnp.log(top * (1.0 / LEVELS)) * LOG2_E)
            levels.append(jnp.round(total * jnp.exp2(-exponent)).astype(I32))
            exponents.append(exponent.astype(I32))
        for i in range(pair):
            packed = (levels[i] << 16) | (levels[i + pair] & 0xFFFF)
            q_out[c, n, i * fields : (i + 1) * fields] = packed
        for i in range(part):
            q_out[c, n, values + i : values + i + 1] = exponents[i]

    arriving = []

    def send(n, c):
        copy = pltpu.make_async_remote_copy(
            src_ref=q_out.at[c, n, used],
            dst_ref=q_in.at[c, 8 - n, used],
            send_sem=send_sem.at[c, n],
            recv_sem=recv_sem.at[c, 8 - n],
            device_id=device(n),
            device_id_type=MESH,
        )
        copy.start()
        arriving[c].append(copy)

    for c in range(PARTS):
        for n in ORDER:
            encode(n, c)
    pl.semaphore_wait(barrier, 8)
    for c in range(PARTS):
        arriving.append([])
        for n in ORDER:
            send(n, c)
    back_copy.start()
    for t in range(tiles):
        import_ref[t] = slot_sum(SELF * tiles + t)
    for copy in small_copies[3:]:
        copy.wait()
    back_order[0:1] = neighbour_keys(
        back_order[0:1], back_order[1:2], row, col, n_row, n_col, tiles
    )
    order_copy = pltpu.make_async_copy(back_order, order_ref, order_sem)
    order_copy.start()

    answers = []
    for c in range(PARTS):
        span = pl.ds(c * part, part)
        for n, copy in zip(ORDER[::-1], arriving[c][::-1]):
            copy.wait_recv()
            for i in range(part):
                packed = q_in[c, 8 - n, (i % pair) * fields : (i % pair + 1) * fields]
                level = packed >> 16 if i < pair else (packed << 16) >> 16
                exponent = q_in[c, 8 - n, values + i : values + i + 1].astype(F32)
                import_ref[c * part + i] = import_ref[c * part + i] + level.astype(F32) * jnp.exp2(exponent)
        for i in range(part):
            t = c * part + i
            wet = mask_ref[t : t + 1].astype(F32)
            near_ref[SELF, t] = (wet * jnp.tanh(state_ref[t] + import_ref[t])).astype(jnp.bfloat16)
        for n in ORDER:
            copy = pltpu.make_async_remote_copy(
                src_ref=near_ref.at[SELF, span],
                dst_ref=near_ref.at[8 - n, span],
                send_sem=resp_send_sem.at[c, n],
                recv_sem=resp_recv_sem.at[c, 8 - n],
                device_id=device(n),
                device_id_type=MESH,
            )
            copy.start()
            answers.append(copy)
    back_copy.wait()
    order_copy.wait()
    for copies in arriving:
        for copy in copies:
            copy.wait_send()
    for copy in answers:
        copy.wait()


def backward(order_ref, near_ref, import_ref, w_ref, imported_ref, out_ref):
    count = order_ref.shape[1]
    atmos, fields, cells = out_ref.shape
    imported_ref[...] = import_ref[...]

    def clear(t, _):
        out_ref[t] = jnp.zeros((fields, cells), F32)
        return 0

    lax.fori_loop(0, atmos, clear, 0, unroll=atmos)

    def two(i, _):
        b = 2 * i
        products = pair_products(
            [near_ref[order_ref[0, b + side]] for side in range(2)],
            [w_ref[b + side] for side in range(2)],
        )
        for side in range(2):
            dst = order_ref[2, b + side]
            out_ref[dst] = out_ref[dst] + products[side]
        return 0

    lax.fori_loop(0, count // 2, two, 0, unroll=count // 2)


def shards(
    atm_fields,
    fwd_blocks,
    fwd_src_tile,
    fwd_dst_dev,
    fwd_dst_tile,
    ocean_state,
    wet_mask,
    back_blocks,
    back_src_dev,
    back_src_tile,
    back_dst_tile,
):
    n_row = lax.axis_size("atm")
    n_col = lax.axis_size("ocn")
    blocks, cells, _ = fwd_blocks.shape
    group = blocks // HALVES
    atmos, fields, _ = atm_fields.shape
    tiles = ocean_state.shape[0]
    rows = tiles // PARTS // 2 * fields + 8
    vmem = pl.BlockSpec(memory_space=pltpu.VMEM)
    smem = pl.BlockSpec(memory_space=pltpu.SMEM)
    hbm = pl.BlockSpec(memory_space=pltpu.HBM)
    ocean_import, near, back_near, order = pl.pallas_call(
        functools.partial(exchange, n_row, n_col),
        out_shape=(
            jax.ShapeDtypeStruct((tiles, fields, cells), F32),
            jax.ShapeDtypeStruct((9, tiles, fields, cells), jnp.bfloat16),
            jax.ShapeDtypeStruct((blocks, cells, cells), jnp.bfloat16),
            pltpu.SMEM((3, blocks), I32),
        ),
        in_specs=[hbm] * 11,
        out_specs=(vmem, vmem, vmem, smem),
        scratch_shapes=[
            pltpu.VMEM((1, blocks), I32),
            pltpu.VMEM((1, blocks), I32),
            pltpu.VMEM((1, blocks), I32),
            pltpu.VMEM((3, blocks), I32),
            pltpu.VMEM((tiles, fields, cells), F32),
            pltpu.VMEM((tiles, cells), I32),
            pltpu.SemaphoreType.DMA((8,)),
            pltpu.SemaphoreType.DMA,
            pltpu.SemaphoreType.DMA,
            pltpu.VMEM((atmos, fields, cells), jnp.bfloat16),
            *[pltpu.VMEM((group, cells, cells), jnp.bfloat16)] * HALVES,
            pltpu.VMEM((blocks, fields, cells), F32),
            pltpu.VMEM((PREP_ROWS, 256), I32),
            pltpu.SMEM((PREP_ROWS, 256), I32),
            pltpu.VMEM((PARTS, 9, rows, cells), I32),
            pltpu.VMEM((PARTS, 9, rows, cells), I32),
            pltpu.SemaphoreType.DMA,
            pltpu.SemaphoreType.DMA((HALVES,)),
            pltpu.SemaphoreType.DMA,
            *[pltpu.SemaphoreType.DMA((PARTS, 9))] * 4,
        ],
        compiler_params=pltpu.CompilerParams(
            collective_id=0, has_side_effects=True, vmem_limit_bytes=28 * 2**20
        ),
        name="exchange",
    )(
        *[
            pltpu.with_memory_space_constraint(operand, pltpu.HBM)
            for operand in (
                fwd_src_tile.reshape(1, blocks),
                fwd_dst_dev.reshape(1, blocks),
                fwd_dst_tile.reshape(1, blocks),
                atm_fields,
                fwd_blocks,
                ocean_state,
                wet_mask,
                back_blocks,
                back_src_dev.reshape(1, blocks),
                back_src_tile.reshape(1, blocks),
                back_dst_tile.reshape(1, blocks),
            )
        ]
    )
    return pl.pallas_call(
        backward,
        out_shape=(
            jax.ShapeDtypeStruct((tiles, fields, cells), F32),
            jax.ShapeDtypeStruct((atmos, fields, cells), F32),
        ),
        in_specs=[smem, vmem, vmem, vmem],
        out_specs=(vmem, vmem),
        compiler_params=pltpu.CompilerParams(vmem_limit_bytes=28 * 2**20),
        name="backward",
    )(
        pltpu.with_memory_space_constraint(order, pltpu.SMEM),
        near.reshape(9 * tiles, fields, cells),
        ocean_import,
        back_near,
    )


def solution(mesh):
    both = ("atm", "ocn")
    in_specs = (
        P(both, None, None),
        P(both, None, None),
        P(both),
        P(both, None),
        P(both),
        P(both, None, None),
        P(both, None),
        P(both, None, None),
        P(both, None),
        P(both),
        P(both),
    )
    out_specs = (P(both, None, None), P(both, None, None))
    return jax.shard_map(shards, mesh=mesh, in_specs=in_specs, out_specs=out_specs, check_vma=False)
```

```python
import functools

import jax
import jax.numpy as jnp
from jax import lax
from jax.experimental import pallas as pl
from jax.experimental.pallas import tpu as pltpu
from jax.sharding import PartitionSpec as P

MESH = pl.DeviceIdType.MESH
I32 = jnp.int32
F32 = jnp.float32
HALVES = 2
PARTS = 2
LEVELS = 32000.0
LOG2_E = 1.4426950408889634
PREP_ROWS = 8
ORDER = (0, 2, 6, 8, 1, 7, 3, 5)
SELF = 4


def steps(n):
    return n // 3 - 1, n % 3 - 1


def neighbour_keys(dev, tile, here_row, here_col, n_row, n_col, tiles):
    shift = n_col.bit_length() - 1
    rel_row = ((dev >> shift) - here_row) & (n_row - 1)
    rel_col = ((dev & (n_col - 1)) - here_col) & (n_col - 1)
    row_step = jnp.where(rel_row == n_row - 1, 0, jnp.where(rel_row == 0, 1, 2))
    col_step = jnp.where(rel_col == n_col - 1, 0, jnp.where(rel_col == 0, 1, 2))
    return (row_step * 3 + col_step) * tiles + tile


def sorted_order(key, src, tiles):
    count = key.shape[1]
    group = count // HALVES
    lane = lax.broadcasted_iota(I32, (1, count), 1)
    half = jnp.zeros_like(lane)
    for h in range(1, HALVES):
        half = half + (lane >= h * group).astype(I32)
    wide_key = half * 128 + key
    rank_row = wide_key * 256 + lane
    eye = lax.broadcasted_iota(I32, (count, count), 0) == lax.broadcasted_iota(
        I32, (count, count), 1
    )

    def column(row):
        return jnp.sum(jnp.where(eye, row, 0), axis=1, keepdims=True)

    rank_col = column(rank_row)
    src_col = column(src)
    place = jnp.sum((rank_row < rank_col).astype(I32), axis=1, keepdims=True)
    lanes = lax.broadcasted_iota(I32, (count, 256), 1)
    hit = place == lanes
    local = (rank_col & 255) - (rank_col >> 15) * group
    key_col = rank_col >> 8

    def arranged(col):
        return jnp.sum(jnp.where(hit, col, 0), axis=0, keepdims=True)

    rows = [arranged(local), arranged(src_col), arranged(key_col)]
    for h in range(HALVES):
        slot = lanes + h * 128
        inside = (key_col == slot) & (lanes < 128)
        upto = jnp.sum((key_col <= slot).astype(I32), axis=0, keepdims=True)
        some = jnp.sum(inside.astype(I32), axis=0, keepdims=True)
        rows.append(jnp.where(some > 0, upto - 1, -1))
    return rows


def pair_products(left, right):
    rows, cols = left[0].shape[0], right[0].shape[1]
    product = jnp.dot(
        jnp.concatenate(left, axis=0),
        jnp.concatenate(right, axis=1),
        preferred_element_type=F32,
    )
    return product[:rows, :cols], product[rows:, cols:]


def by_destination(slot, dst):
    count = dst.shape[1]
    square = (count, count)
    lane = lax.broadcasted_iota(I32, square, 1)
    eye = lax.broadcasted_iota(I32, square, 0) == lane
    rank_row = dst * 256 + lane[:1]

    def column(row):
        return jnp.sum(jnp.where(eye, row, 0), axis=1, keepdims=True)

    rank_col = column(rank_row)
    place = jnp.sum((rank_row < rank_col).astype(I32), axis=1, keepdims=True)
    hit = place == lane
    return [
        jnp.sum(jnp.where(hit, col, 0), axis=0, keepdims=True)
        for col in (column(slot), rank_col & 255, rank_col >> 8)
    ]


def exchange(
    n_row,
    n_col,
    src_hbm,
    dev_hbm,
    tile_hbm,
    atm_hbm,
    w_hbm,
    state_hbm,
    mask_hbm,
    back_hbm,
    back_dev_hbm,
    back_tile_hbm,
    back_dst_hbm,
    import_ref,
    near_ref,
    back_ref,
    order_ref,
    src_ref,
    dev_ref,
    tile_ref,
    back_order,
    state_ref,
    mask_ref,
    small_sem,
    order_sem,
    back_sem,
    atm_v,
    *scratch,
):
    w_v = scratch[:HALVES]
    (
        sums,
        prep_v,
        prep_s,
        q_out,
            q_in,
        atm_sem,
        w_sem,
        prep_sem,
        send_sem,
        recv_sem,
        resp_send_sem,
        resp_recv_sem,
    ) = scratch[HALVES:]
    count = dev_ref.shape[1]
    group = count // HALVES
    tiles, fields, cells = state_ref.shape
    row = lax.axis_index("atm")
    col = lax.axis_index("ocn")

    def device(n):
        dr, dc = steps(n)
        return (lax.rem(row + dr + n_row, n_row), lax.rem(col + dc + n_col, n_col))

    def w_copy(h):
        return pltpu.make_async_copy(
            w_hbm.at[pl.ds(h * group, group)], w_v[h], w_sem.at[h]
        )

    barrier = pltpu.get_barrier_semaphore()
    for n in ORDER:
        pl.semaphore_signal(barrier, inc=1, device_id=device(n), device_id_type=MESH)

    w_copy(0).start()
    small_copies = [
        pltpu.make_async_copy(source, target, small_sem.at[i])
        for i, (source, target) in enumerate(
            (
                (src_hbm, src_ref),
                (dev_hbm, dev_ref),
                (tile_hbm, tile_ref),
                (state_hbm, state_ref),
                (mask_hbm, mask_ref),
                (back_dev_hbm, back_order.at[pl.ds(0, 1)]),
                (back_tile_hbm, back_order.at[pl.ds(1, 1)]),
                (back_dst_hbm, back_order.at[pl.ds(2, 1)]),
            )
        )
    ]
    for copy in small_copies[:3]:
        copy.start()
    atm_copy = pltpu.make_async_copy(atm_hbm, atm_v, atm_sem)
    atm_copy.start()
    for copy in small_copies[:3]:
        copy.wait()
    key = neighbour_keys(dev_ref[...], tile_ref[...], row, col, n_row, n_col, tiles)
    rows = sorted_order(key, src_ref[...], tiles)
    for i, values in enumerate(rows):
        prep_v[i : i + 1, :] = values
    prep_copy = pltpu.make_async_copy(prep_v, prep_s, prep_sem)
    prep_copy.start()
    for h in range(1, HALVES):
        w_copy(h).start()
    for copy in small_copies[3:]:
        copy.start()
    prep_copy.wait()
    atm_copy.wait()

    back_copy = pltpu.make_async_copy(back_hbm, back_ref, back_sem)
    for h in range(HALVES):
        w_copy(h).wait()

        def two(i, total, h=h):
            k = h * group + 2 * i
            products = pair_products(
                [atm_v[prep_s[1, k + side]] for side in range(2)],
                [w_v[h][prep_s[0, k + side]] for side in range(2)],
            )
            for side in range(2):
                before = prep_s[2, jnp.maximum(k + side - 1, 0)]
                same = (prep_s[2, k + side] == before) & (2 * i + side > 0)
                keep = jnp.where(same, 1.0, 0.0).astype(F32)
                total = total * keep + products[side]
                sums[k + side] = total
            return total

        lax.fori_loop(
            0, group // 2, two, jnp.zeros((fields, cells), F32), unroll=group // 2
        )

    def slot_sum(slot):
        total = None
        for h in range(HALVES):
            last = prep_s[3 + h, slot]
            part = sums[jnp.maximum(last, 0)] * jnp.where(last >= 0, 1.0, 0.0).astype(F32)
            total = part if total is None else total + part
        return total

    part = tiles // PARTS
    pair = part // 2
    values = pair * fields
    used = pl.ds(0, values + part)

    def encode(n, c):
        exponents = []
        levels = []
        for i in range(part):
            total = slot_sum(n * tiles + c * part + i)
            top = jnp.maximum(jnp.max(jnp.abs(total), axis=0, keepdims=True), 1e-30)
            exponent = jnp.ceil(jnp.log(top * (1.0 / LEVELS)) * LOG2_E)
            levels.append(jnp.round(total * jnp.exp2(-exponent)).astype(I32))
            exponents.append(exponent.astype(I32))
        for i in range(pair):
            packed = (levels[i] << 16) | (levels[i + pair] & 0xFFFF)
            q_out[c, n, i * fields : (i + 1) * fields] = packed
        for i in range(part):
            q_out[c, n, values + i : values + i + 1] = exponents[i]

    arriving = []

    def send(n, c):
        copy = pltpu.make_async_remote_copy(
            src_ref=q_out.at[c, n, used],
            dst_ref=q_in.at[c, 8 - n, used],
            send_sem=send_sem.at[c, n],
            recv_sem=recv_sem.at[c, 8 - n],
            device_id=device(n),
            device_id_type=MESH,
        )
        copy.start()
        arriving[c].append(copy)

    for c in range(PARTS):
        for n in ORDER:
            encode(n, c)
    pl.semaphore_wait(barrier, 8)
    for c in range(PARTS):
        arriving.append([])
        for n in ORDER:
            send(n, c)
    back_copy.start()
    for t in range(tiles):
        import_ref[t] = slot_sum(SELF * tiles + t)
    for copy in small_copies[3:]:
        copy.wait()
    slots = neighbour_keys(
        back_order[0:1], back_order[1:2], row, col, n_row, n_col, tiles
    )
    for i, values_row in enumerate(by_destination(slots, back_order[2:3])):
        back_order[i : i + 1] = values_row
    order_copy = pltpu.make_async_copy(back_order, order_ref, order_sem)
    order_copy.start()

    answers = []
    for c in range(PARTS):
        span = pl.ds(c * part, part)
        for n, copy in zip(ORDER[::-1], arriving[c][::-1]):
            copy.wait_recv()
            for i in range(part):
                packed = q_in[c, 8 - n, (i % pair) * fields : (i % pair + 1) * fields]
                level = packed >> 16 if i < pair else (packed << 16) >> 16
                exponent = q_in[c, 8 - n, values + i : values + i + 1].astype(F32)
                import_ref[c * part + i] = import_ref[c * part + i] + level.astype(F32) * jnp.exp2(exponent)
        for i in range(part):
            t = c * part + i
            wet = mask_ref[t : t + 1].astype(F32)
            near_ref[SELF, t] = (wet * jnp.tanh(state_ref[t] + import_ref[t])).astype(jnp.bfloat16)
        for n in ORDER:
            copy = pltpu.make_async_remote_copy(
                src_ref=near_ref.at[SELF, span],
                dst_ref=near_ref.at[8 - n, span],
                send_sem=resp_send_sem.at[c, n],
                recv_sem=resp_recv_sem.at[c, 8 - n],
                device_id=device(n),
                device_id_type=MESH,
            )
            copy.start()
            answers.append(copy)
    back_copy.wait()
    order_copy.wait()
    for copies in arriving:
        for copy in copies:
            copy.wait_send()
    for copy in answers:
        copy.wait()


def backward(order_ref, near_ref, import_ref, w_ref, imported_hbm, out_hbm, out_ref, sem):
    count = order_ref.shape[1]
    atmos, fields, cells = out_ref.shape
    import_copy = pltpu.make_async_copy(import_ref, imported_hbm, sem.at[0])
    import_copy.start()

    def clear(t, _):
        out_ref[t] = jnp.zeros((fields, cells), F32)
        return 0

    lax.fori_loop(0, atmos, clear, 0, unroll=atmos)

    def two(i, _):
        b = 2 * i
        products = pair_products(
            [near_ref[order_ref[0, b + side]] for side in range(2)],
            [w_ref[order_ref[1, b + side]] for side in range(2)],
        )
        for side in range(2):
            dst = order_ref[2, b + side]
            out_ref[dst] = out_ref[dst] + products[side]
        return 0

    quarter = atmos // 4
    out_copies = [
        pltpu.make_async_copy(
            out_ref.at[pl.ds(q * quarter, quarter)],
            out_hbm.at[pl.ds(q * quarter, quarter)],
            sem.at[1 + q],
        )
        for q in range(4)
    ]
    first = count // 3
    lax.fori_loop(0, first, two, 0, unroll=first)
    ready = order_ref[2, 2 * first]
    for q, copy in enumerate(out_copies):
        pl.when(ready >= (q + 1) * quarter)(copy.start)
    lax.fori_loop(first, count // 2, two, 0, unroll=count // 2 - first)
    for q, copy in enumerate(out_copies):
        pl.when(ready < (q + 1) * quarter)(copy.start)
    for copy in [import_copy, *out_copies]:
        copy.wait()


def shards(
    atm_fields,
    fwd_blocks,
    fwd_src_tile,
    fwd_dst_dev,
    fwd_dst_tile,
    ocean_state,
    wet_mask,
    back_blocks,
    back_src_dev,
    back_src_tile,
    back_dst_tile,
):
    n_row = lax.axis_size("atm")
    n_col = lax.axis_size("ocn")
    blocks, cells, _ = fwd_blocks.shape
    group = blocks // HALVES
    atmos, fields, _ = atm_fields.shape
    tiles = ocean_state.shape[0]
    rows = tiles // PARTS // 2 * fields + 8
    vmem = pl.BlockSpec(memory_space=pltpu.VMEM)
    smem = pl.BlockSpec(memory_space=pltpu.SMEM)
    hbm = pl.BlockSpec(memory_space=pltpu.HBM)
    ocean_import, near, back_near, order = pl.pallas_call(
        functools.partial(exchange, n_row, n_col),
        out_shape=(
            jax.ShapeDtypeStruct((tiles, fields, cells), F32),
            jax.ShapeDtypeStruct((9, tiles, fields, cells), jnp.bfloat16),
            jax.ShapeDtypeStruct((blocks, cells, cells), jnp.bfloat16),
            pltpu.SMEM((3, blocks), I32),
        ),
        in_specs=[hbm] * 11,
        out_specs=(vmem, vmem, vmem, smem),
        scratch_shapes=[
            pltpu.VMEM((1, blocks), I32),
            pltpu.VMEM((1, blocks), I32),
            pltpu.VMEM((1, blocks), I32),
            pltpu.VMEM((3, blocks), I32),
            pltpu.VMEM((tiles, fields, cells), F32),
            pltpu.VMEM((tiles, cells), I32),
            pltpu.SemaphoreType.DMA((8,)),
            pltpu.SemaphoreType.DMA,
            pltpu.SemaphoreType.DMA,
            pltpu.VMEM((atmos, fields, cells), jnp.bfloat16),
            *[pltpu.VMEM((group, cells, cells), jnp.bfloat16)] * HALVES,
            pltpu.VMEM((blocks, fields, cells), F32),
            pltpu.VMEM((PREP_ROWS, 256), I32),
            pltpu.SMEM((PREP_ROWS, 256), I32),
            pltpu.VMEM((PARTS, 9, rows, cells), I32),
            pltpu.VMEM((PARTS, 9, rows, cells), I32),
            pltpu.SemaphoreType.DMA,
            pltpu.SemaphoreType.DMA((HALVES,)),
            pltpu.SemaphoreType.DMA,
            *[pltpu.SemaphoreType.DMA((PARTS, 9))] * 4,
        ],
        compiler_params=pltpu.CompilerParams(
            collective_id=0, has_side_effects=True, vmem_limit_bytes=28 * 2**20
        ),
        name="exchange",
    )(
        *[
            pltpu.with_memory_space_constraint(operand, pltpu.HBM)
            for operand in (
                fwd_src_tile.reshape(1, blocks),
                fwd_dst_dev.reshape(1, blocks),
                fwd_dst_tile.reshape(1, blocks),
                atm_fields,
                fwd_blocks,
                ocean_state,
                wet_mask,
                back_blocks,
                back_src_dev.reshape(1, blocks),
                back_src_tile.reshape(1, blocks),
                back_dst_tile.reshape(1, blocks),
            )
        ]
    )
    return pl.pallas_call(
        backward,
        out_shape=(
            jax.ShapeDtypeStruct((tiles, fields, cells), F32),
            jax.ShapeDtypeStruct((atmos, fields, cells), F32),
        ),
        in_specs=[smem, vmem, vmem, vmem],
        out_specs=(hbm, hbm),
        scratch_shapes=[
            pltpu.VMEM((atmos, fields, cells), F32),
            pltpu.SemaphoreType.DMA((5,)),
        ],
        compiler_params=pltpu.CompilerParams(vmem_limit_bytes=28 * 2**20),
        name="backward",
    )(
        pltpu.with_memory_space_constraint(order, pltpu.SMEM),
        near.reshape(9 * tiles, fields, cells),
        ocean_import,
        back_near,
    )


def solution(mesh):
    both = ("atm", "ocn")
    in_specs = (
        P(both, None, None),
        P(both, None, None),
        P(both),
        P(both, None),
        P(both),
        P(both, None, None),
        P(both, None),
        P(both, None, None),
        P(both, None),
        P(both),
        P(both),
    )
    out_specs = (P(both, None, None), P(both, None, None))
    return jax.shard_map(shards, mesh=mesh, in_specs=in_specs, out_specs=out_specs, check_vma=False)
```

```python
import functools

import jax
import jax.numpy as jnp
from jax import lax
from jax.experimental import pallas as pl
from jax.experimental.pallas import tpu as pltpu
from jax.sharding import PartitionSpec as P

MESH = pl.DeviceIdType.MESH
I32 = jnp.int32
F32 = jnp.float32
HALVES = 2
PARTS = 2
LEVELS = 32000.0
LOG2_E = 1.4426950408889634
PREP_ROWS = 8
ORDER = (0, 2, 6, 8, 1, 7, 3, 5)
SELF = 4
SHARES = 8


def steps(n):
    return n // 3 - 1, n % 3 - 1


def neighbour_keys(dev, tile, here_row, here_col, n_row, n_col, tiles):
    shift = n_col.bit_length() - 1
    rel_row = ((dev >> shift) - here_row) & (n_row - 1)
    rel_col = ((dev & (n_col - 1)) - here_col) & (n_col - 1)
    row_step = jnp.where(rel_row == n_row - 1, 0, jnp.where(rel_row == 0, 1, 2))
    col_step = jnp.where(rel_col == n_col - 1, 0, jnp.where(rel_col == 0, 1, 2))
    return (row_step * 3 + col_step) * tiles + tile


def sorted_order(key, src, tiles):
    count = key.shape[1]
    group = count // HALVES
    lane = lax.broadcasted_iota(I32, (1, count), 1)
    half = jnp.zeros_like(lane)
    for h in range(1, HALVES):
        half = half + (lane >= h * group).astype(I32)
    wide_key = half * 128 + key
    rank_row = wide_key * 256 + lane
    eye = lax.broadcasted_iota(I32, (count, count), 0) == lax.broadcasted_iota(
        I32, (count, count), 1
    )

    def column(row):
        return jnp.sum(jnp.where(eye, row, 0), axis=1, keepdims=True)

    rank_col = column(rank_row)
    src_col = column(src)
    place = jnp.sum((rank_row < rank_col).astype(I32), axis=1, keepdims=True)
    lanes = lax.broadcasted_iota(I32, (count, 256), 1)
    hit = place == lanes
    local = (rank_col & 255) - (rank_col >> 15) * group
    key_col = rank_col >> 8

    def arranged(col):
        return jnp.sum(jnp.where(hit, col, 0), axis=0, keepdims=True)

    rows = [arranged(local), arranged(src_col), arranged(key_col)]
    for h in range(HALVES):
        slot = lanes + h * 128
        inside = (key_col == slot) & (lanes < 128)
        upto = jnp.sum((key_col <= slot).astype(I32), axis=0, keepdims=True)
        some = jnp.sum(inside.astype(I32), axis=0, keepdims=True)
        rows.append(jnp.where(some > 0, upto - 1, -1))
    return rows


def pair_products(left, right):
    rows, cols = left[0].shape[0], right[0].shape[1]
    product = jnp.dot(
        jnp.concatenate(left, axis=0),
        jnp.concatenate(right, axis=1),
        preferred_element_type=F32,
    )
    return product[:rows, :cols], product[rows:, cols:]


def by_destination(slot, dst):
    count = dst.shape[1]
    square = (count, count)
    lane = lax.broadcasted_iota(I32, square, 1)
    eye = lax.broadcasted_iota(I32, square, 0) == lane
    rank_row = dst * 256 + lane[:1]

    def column(row):
        return jnp.sum(jnp.where(eye, row, 0), axis=1, keepdims=True)

    rank_col = column(rank_row)
    place = jnp.sum((rank_row < rank_col).astype(I32), axis=1, keepdims=True)
    hit = place == lane
    return [
        jnp.sum(jnp.where(hit, col, 0), axis=0, keepdims=True)
        for col in (column(slot), rank_col & 255, rank_col >> 8)
    ]


def exchange(
    n_row,
    n_col,
    src_hbm,
    dev_hbm,
    tile_hbm,
    atm_hbm,
    w_hbm,
    state_hbm,
    mask_hbm,
    back_hbm,
    back_dev_hbm,
    back_tile_hbm,
    back_dst_hbm,
    import_ref,
    near_ref,
    back_ref,
    order_ref,
    src_ref,
    dev_ref,
    tile_ref,
    back_order,
    state_ref,
    mask_ref,
    small_sem,
    order_sem,
    back_sem,
    atm_v,
    *scratch,
):
    w_v = scratch[:HALVES]
    (
        sums,
        prep_v,
        prep_s,
        q_out,
            q_in,
        atm_sem,
        w_sem,
        prep_sem,
        send_sem,
        recv_sem,
        resp_send_sem,
        resp_recv_sem,
    ) = scratch[HALVES:]
    count = dev_ref.shape[1]
    group = count // HALVES
    tiles, fields, cells = state_ref.shape
    row = lax.axis_index("atm")
    col = lax.axis_index("ocn")

    def device(n):
        dr, dc = steps(n)
        return (lax.rem(row + dr + n_row, n_row), lax.rem(col + dc + n_col, n_col))

    def w_copy(h):
        return pltpu.make_async_copy(
            w_hbm.at[pl.ds(h * group, group)], w_v[h], w_sem.at[h]
        )

    barrier = pltpu.get_barrier_semaphore()
    for n in ORDER:
        pl.semaphore_signal(barrier, inc=1, device_id=device(n), device_id_type=MESH)

    w_copy(0).start()
    small_copies = [
        pltpu.make_async_copy(source, target, small_sem.at[i])
        for i, (source, target) in enumerate(
            (
                (src_hbm, src_ref),
                (dev_hbm, dev_ref),
                (tile_hbm, tile_ref),
                (state_hbm, state_ref),
                (mask_hbm, mask_ref),
                (back_dev_hbm, back_order.at[pl.ds(0, 1)]),
                (back_tile_hbm, back_order.at[pl.ds(1, 1)]),
                (back_dst_hbm, back_order.at[pl.ds(2, 1)]),
            )
        )
    ]
    for copy in small_copies[:3]:
        copy.start()
    atm_copy = pltpu.make_async_copy(atm_hbm, atm_v, atm_sem)
    atm_copy.start()
    for copy in small_copies[:3]:
        copy.wait()
    key = neighbour_keys(dev_ref[...], tile_ref[...], row, col, n_row, n_col, tiles)
    rows = sorted_order(key, src_ref[...], tiles)
    for i, values in enumerate(rows):
        prep_v[i : i + 1, :] = values
    prep_copy = pltpu.make_async_copy(prep_v, prep_s, prep_sem)
    prep_copy.start()
    for h in range(1, HALVES):
        w_copy(h).start()
    for copy in small_copies[3:]:
        copy.start()
    prep_copy.wait()
    atm_copy.wait()

    back_copy = pltpu.make_async_copy(back_hbm, back_ref, back_sem)
    for h in range(HALVES):
        w_copy(h).wait()

        def two(i, total, h=h):
            k = h * group + 2 * i
            products = pair_products(
                [atm_v[prep_s[1, k + side]] for side in range(2)],
                [w_v[h][prep_s[0, k + side]] for side in range(2)],
            )
            for side in range(2):
                before = prep_s[2, jnp.maximum(k + side - 1, 0)]
                same = (prep_s[2, k + side] == before) & (2 * i + side > 0)
                keep = jnp.where(same, 1.0, 0.0).astype(F32)
                total = total * keep + products[side]
                sums[k + side] = total
            return total

        lax.fori_loop(
            0, group // 2, two, jnp.zeros((fields, cells), F32), unroll=group // 2
        )

    def slot_sum(slot):
        total = None
        for h in range(HALVES):
            last = prep_s[3 + h, slot]
            part = sums[jnp.maximum(last, 0)] * jnp.where(last >= 0, 1.0, 0.0).astype(F32)
            total = part if total is None else total + part
        return total

    part = tiles // PARTS
    pair = part // 2
    values = pair * fields
    used = pl.ds(0, values + part)

    def encode(n, c):
        exponents = []
        levels = []
        for i in range(part):
            total = slot_sum(n * tiles + c * part + i)
            top = jnp.maximum(jnp.max(jnp.abs(total), axis=0, keepdims=True), 1e-30)
            exponent = jnp.ceil(jnp.log(top * (1.0 / LEVELS)) * LOG2_E)
            levels.append(jnp.round(total * jnp.exp2(-exponent)).astype(I32))
            exponents.append(exponent.astype(I32))
        for i in range(pair):
            packed = (levels[i] << 16) | (levels[i + pair] & 0xFFFF)
            q_out[c, n, i * fields : (i + 1) * fields] = packed
        for i in range(part):
            q_out[c, n, values + i : values + i + 1] = exponents[i]

    arriving = []

    def send(n, c):
        copy = pltpu.make_async_remote_copy(
            src_ref=q_out.at[c, n, used],
            dst_ref=q_in.at[c, 8 - n, used],
            send_sem=send_sem.at[c, n],
            recv_sem=recv_sem.at[c, 8 - n],
            device_id=device(n),
            device_id_type=MESH,
        )
        copy.start()
        arriving[c].append(copy)

    for c in range(PARTS):
        for n in ORDER:
            encode(n, c)
    pl.semaphore_wait(barrier, 8)
    for c in range(PARTS):
        arriving.append([])
        for n in ORDER:
            send(n, c)
    back_copy.start()
    for t in range(tiles):
        import_ref[t] = slot_sum(SELF * tiles + t)
    for copy in small_copies[3:]:
        copy.wait()
    slots = neighbour_keys(
        back_order[0:1], back_order[1:2], row, col, n_row, n_col, tiles
    )
    for i, values_row in enumerate(by_destination(slots, back_order[2:3])):
        back_order[i : i + 1] = values_row
    order_copy = pltpu.make_async_copy(back_order, order_ref, order_sem)
    order_copy.start()

    answers = []
    for c in range(PARTS):
        span = pl.ds(c * part, part)
        for n, copy in zip(ORDER[::-1], arriving[c][::-1]):
            copy.wait_recv()
            for i in range(part):
                packed = q_in[c, 8 - n, (i % pair) * fields : (i % pair + 1) * fields]
                level = packed >> 16 if i < pair else (packed << 16) >> 16
                exponent = q_in[c, 8 - n, values + i : values + i + 1].astype(F32)
                import_ref[c * part + i] = import_ref[c * part + i] + level.astype(F32) * jnp.exp2(exponent)
        for i in range(part):
            t = c * part + i
            wet = mask_ref[t : t + 1].astype(F32)
            near_ref[SELF, t] = (wet * jnp.tanh(state_ref[t] + import_ref[t])).astype(jnp.bfloat16)
        for n in ORDER:
            copy = pltpu.make_async_remote_copy(
                src_ref=near_ref.at[SELF, span],
                dst_ref=near_ref.at[8 - n, span],
                send_sem=resp_send_sem.at[c, n],
                recv_sem=resp_recv_sem.at[c, 8 - n],
                device_id=device(n),
                device_id_type=MESH,
            )
            copy.start()
            answers.append(copy)
    back_copy.wait()
    order_copy.wait()
    for copies in arriving:
        for copy in copies:
            copy.wait_send()
    for copy in answers:
        copy.wait()


def backward(order_ref, near_ref, import_ref, w_ref, imported_hbm, out_hbm, out_ref, sem):
    count = order_ref.shape[1]
    atmos, fields, cells = out_ref.shape
    import_copy = pltpu.make_async_copy(import_ref, imported_hbm, sem.at[0])
    import_copy.start()

    def clear(t, _):
        out_ref[t] = jnp.zeros((fields, cells), F32)
        return 0

    lax.fori_loop(0, atmos, clear, 0, unroll=atmos)

    def two(i, _):
        b = 2 * i
        products = pair_products(
            [near_ref[order_ref[0, b + side]] for side in range(2)],
            [w_ref[order_ref[1, b + side]] for side in range(2)],
        )
        for side in range(2):
            dst = order_ref[2, b + side]
            out_ref[dst] = out_ref[dst] + products[side]
        return 0

    share = atmos // SHARES
    out_copies = [
        pltpu.make_async_copy(
            out_ref.at[pl.ds(q * share, share)],
            out_hbm.at[pl.ds(q * share, share)],
            sem.at[1 + q],
        )
        for q in range(SHARES)
    ]
    first = count * 3 // 8
    lax.fori_loop(0, first, two, 0, unroll=first)
    ready = order_ref[2, 2 * first]
    for q, copy in enumerate(out_copies):
        pl.when(ready >= (q + 1) * share)(copy.start)
    lax.fori_loop(first, count // 2, two, 0, unroll=count // 2 - first)
    for q, copy in enumerate(out_copies):
        pl.when(ready < (q + 1) * share)(copy.start)
    for copy in [import_copy, *out_copies]:
        copy.wait()


def shards(
    atm_fields,
    fwd_blocks,
    fwd_src_tile,
    fwd_dst_dev,
    fwd_dst_tile,
    ocean_state,
    wet_mask,
    back_blocks,
    back_src_dev,
    back_src_tile,
    back_dst_tile,
):
    n_row = lax.axis_size("atm")
    n_col = lax.axis_size("ocn")
    blocks, cells, _ = fwd_blocks.shape
    group = blocks // HALVES
    atmos, fields, _ = atm_fields.shape
    tiles = ocean_state.shape[0]
    rows = tiles // PARTS // 2 * fields + 8
    vmem = pl.BlockSpec(memory_space=pltpu.VMEM)
    smem = pl.BlockSpec(memory_space=pltpu.SMEM)
    hbm = pl.BlockSpec(memory_space=pltpu.HBM)
    ocean_import, near, back_near, order = pl.pallas_call(
        functools.partial(exchange, n_row, n_col),
        out_shape=(
            jax.ShapeDtypeStruct((tiles, fields, cells), F32),
            jax.ShapeDtypeStruct((9, tiles, fields, cells), jnp.bfloat16),
            jax.ShapeDtypeStruct((blocks, cells, cells), jnp.bfloat16),
            pltpu.SMEM((3, blocks), I32),
        ),
        in_specs=[hbm] * 11,
        out_specs=(vmem, vmem, vmem, smem),
        scratch_shapes=[
            pltpu.VMEM((1, blocks), I32),
            pltpu.VMEM((1, blocks), I32),
            pltpu.VMEM((1, blocks), I32),
            pltpu.VMEM((3, blocks), I32),
            pltpu.VMEM((tiles, fields, cells), F32),
            pltpu.VMEM((tiles, cells), I32),
            pltpu.SemaphoreType.DMA((8,)),
            pltpu.SemaphoreType.DMA,
            pltpu.SemaphoreType.DMA,
            pltpu.VMEM((atmos, fields, cells), jnp.bfloat16),
            *[pltpu.VMEM((group, cells, cells), jnp.bfloat16)] * HALVES,
            pltpu.VMEM((blocks, fields, cells), F32),
            pltpu.VMEM((PREP_ROWS, 256), I32),
            pltpu.SMEM((PREP_ROWS, 256), I32),
            pltpu.VMEM((PARTS, 9, rows, cells), I32),
            pltpu.VMEM((PARTS, 9, rows, cells), I32),
            pltpu.SemaphoreType.DMA,
            pltpu.SemaphoreType.DMA((HALVES,)),
            pltpu.SemaphoreType.DMA,
            *[pltpu.SemaphoreType.DMA((PARTS, 9))] * 4,
        ],
        compiler_params=pltpu.CompilerParams(
            collective_id=0, has_side_effects=True, vmem_limit_bytes=28 * 2**20
        ),
        name="exchange",
    )(
        *[
            pltpu.with_memory_space_constraint(operand, pltpu.HBM)
            for operand in (
                fwd_src_tile.reshape(1, blocks),
                fwd_dst_dev.reshape(1, blocks),
                fwd_dst_tile.reshape(1, blocks),
                atm_fields,
                fwd_blocks,
                ocean_state,
                wet_mask,
                back_blocks,
                back_src_dev.reshape(1, blocks),
                back_src_tile.reshape(1, blocks),
                back_dst_tile.reshape(1, blocks),
            )
        ]
    )
    return pl.pallas_call(
        backward,
        out_shape=(
            jax.ShapeDtypeStruct((tiles, fields, cells), F32),
            jax.ShapeDtypeStruct((atmos, fields, cells), F32),
        ),
        in_specs=[smem, vmem, vmem, vmem],
        out_specs=(hbm, hbm),
        scratch_shapes=[
            pltpu.VMEM((atmos, fields, cells), F32),
            pltpu.SemaphoreType.DMA((1 + SHARES,)),
        ],
        compiler_params=pltpu.CompilerParams(vmem_limit_bytes=28 * 2**20),
        name="backward",
    )(
        pltpu.with_memory_space_constraint(order, pltpu.SMEM),
        near.reshape(9 * tiles, fields, cells),
        ocean_import,
        back_near,
    )


def solution(mesh):
    both = ("atm", "ocn")
    in_specs = (
        P(both, None, None),
        P(both, None, None),
        P(both),
        P(both, None),
        P(both),
        P(both, None, None),
        P(both, None),
        P(both, None, None),
        P(both, None),
        P(both),
        P(both),
    )
    out_specs = (P(both, None, None), P(both, None, None))
    return jax.shard_map(shards, mesh=mesh, in_specs=in_specs, out_specs=out_specs, check_vma=False)
```
